32 devices in a mesh: row: 4 (over y, core), col: 8 (over z, x).
Axes of the slice: x: 2, y: 2, z: 4, core: 2. Of those that a mesh axis runs over, the one named last changes fastest.
Arguments:
- jacobian: bfloat16 [4096, 512], P('row', 'col'), may hold values from -6 to 6
- gram_old: float32 [4096, 4096], P('row', 'col'), may hold values from -1 to 5, as said below
Outputs:
- gram_new: float32 [4096, 4096], P('row', 'col')
- panel_t: float32 [1024, 4096], P('col', 'row')
The draws below stay inside these ranges and needn't reach their ends.
Inputs may be any that keep to these rules, and one draw needn't show every extreme that they name: `gram_old`: symmetric and positive definite with smallest eigenvalue at least 0.5; diagonal entries between 1 and 5, off-diagonal entries at most 4 / sqrt(4096) in magnitude.
All inputs are finite; a program needn't handle non-finite values.
Results may differ from the reference program's by a relative error of at most 0.0003.
Values may be sent and summed in bfloat16 or wider, within the bound.
A program may use at most 128 MiB of HBM per device.

```python
import math
import jax
import jax.numpy as jnp
from jax import lax

PARAMS = 512
PANEL = 1024
SAMPLES = 4096


def draw_gram_old(key, part):
    key_off, key_diag = jax.random.split(jax.random.fold_in(key, 17))
    spread = 0.5
    low_diag = 1.5
    high_diag = 3.0
    base = jnp.clip(jax.random.normal(key_off, (SAMPLES, SAMPLES), jnp.float32), -4.0, 4.0)
    base = base * (spread / jnp.sqrt(2.0 * SAMPLES))
    symmetric = base + base.T
    diagonal = jax.random.uniform(key_diag, (SAMPLES,), jnp.float32, low_diag, high_diag)
    positions = jnp.arange(SAMPLES, dtype=jnp.int32)
    return symmetric.at[positions, positions].set(diagonal)


def draw_jacobian(key, part):
    key_chain, key_fresh = jax.random.split(jax.random.fold_in(key, 29))
    persist = 0.95
    chained = 0.8
    innovations = jax.random.normal(key_chain, (SAMPLES, PARAMS), jnp.float32)
    fresh = jax.random.normal(key_fresh, (SAMPLES, PARAMS), jnp.float32)
    kick = math.sqrt(1.0 - persist * persist)

    def advance(state, noise):
        following = persist * state + kick * noise
        return (following, following)
    first = innovations[0]
    last_state, later = lax.scan(advance, first, innovations[1:])
    chain = jnp.concatenate([first[None, :], later], axis=0)
    values = math.sqrt(chained) * chain + math.sqrt(1.0 - chained) * fresh
    return jnp.clip(values, -6.0, 6.0).astype(jnp.bfloat16)


def setup_inputs(seed: int = 0) -> dict:
    keys = jax.random.split(jax.random.key(seed), 3)
    jacobian = draw_jacobian(jax.random.fold_in(keys[2], 71), 0)
    gram_old = draw_gram_old(jax.random.fold_in(keys[2], 71), 0)
    return {"jacobian": jacobian, "gram_old": gram_old}


def reference(jacobian, gram_old):
    col_ids = jnp.arange(SAMPLES, dtype=jnp.int32)

    def one_block(block_index):
        begin_row = (block_index * PANEL).astype(jnp.int32)
        block_rows = lax.dynamic_slice_in_dim(jacobian, begin_row, PANEL, 0)
        old_rows = lax.dynamic_slice_in_dim(gram_old, begin_row, PANEL, 0)
        product = lax.dot_general(block_rows.astype(jnp.float32), jacobian.astype(jnp.float32), (((1,), (1,)), ((), ())), preferred_element_type=jnp.float32)
        keep_mask = col_ids // PANEL <= block_index
        return jnp.where(keep_mask[None, :], old_rows + product / PARAMS, old_rows)
    gram_new = lax.map(one_block, jnp.arange(SAMPLES // PANEL, dtype=jnp.int32)).reshape(SAMPLES, SAMPLES)
    factor = jnp.linalg.cholesky(gram_new[:PANEL, :PANEL])
    inverse = jax.scipy.linalg.solve_triangular(factor, jnp.eye(PANEL, dtype=factor.dtype), lower=True)
    panel_t = jnp.dot(inverse, gram_new[:, :PANEL].T, precision=lax.Precision.HIGHEST)
    return (gram_new, panel_t)
```

```python
import functools
import jax
import jax.numpy as jnp
from jax import lax
from jax.experimental import pallas as pl
from jax.experimental.pallas import tpu as pltpu
from jax.sharding import PartitionSpec as P

PARAMS = 512
PANEL = 1024
BLOCK = 128


def split3(x):
    high = x.astype(jnp.bfloat16).astype(jnp.float32)
    rest = x - high
    mid = rest.astype(jnp.bfloat16).astype(jnp.float32)
    return high, mid, rest - mid


def left6(x, axis):
    h, m, l = split3(x)
    return jnp.concatenate([h, h, m, h, l, m], axis=axis).astype(jnp.bfloat16)


def right6(x):
    h, m, l = split3(x)
    return jnp.concatenate([h, m, h, l, h, m], axis=0).astype(jnp.bfloat16)


def dot_t(a, b):
    return lax.dot_general(a, b, (((0,), (0,)), ((), ())), preferred_element_type=jnp.float32)


def eliminate(work, sub):
    size = work.shape[0]
    lanes = lax.broadcasted_iota(jnp.int32, (sub, size), 1)
    subs = lax.broadcasted_iota(jnp.int32, (sub, size), 0)
    for start in range(0, size, sub):
        rows = work[start:start + sub, :]
        scale = jnp.ones((sub, size), jnp.float32)
        for i in range(sub):
            at = start + i
            column = jnp.broadcast_to(rows[:, at:at + 1], (sub, size))
            pivot = jnp.broadcast_to(column[i:i + 1, :], (sub, size))
            pivot_row = jnp.where(lanes == at, 1.0, jnp.broadcast_to(rows[i:i + 1, :], (sub, size)))
            factor = jnp.where(subs > i, column * (1.0 / pivot), 0.0)
            kept = jnp.where((lanes == at) & (subs >= i), jnp.where(subs == i, 1.0, 0.0), rows)
            rows = kept - factor * pivot_row
            root = lax.rsqrt(pivot)
            root = root * (1.5 - 0.5 * pivot * root * root)
            scale = jnp.where(subs == i, root, scale)
        rows = rows * scale
        work[start:start + sub, :] = rows
        low = start + sub
        if low < size:
            above = (lanes > subs + start) & (lanes < low)
            update = dot_t(left6(rows, 0), right6(jnp.where(above, 0.0, rows)))
            wide = lax.broadcasted_iota(jnp.int32, (size - low, size), 1)
            inside = (wide >= start) & (wide < low)
            work[low:, :] = jnp.where(inside, 0.0, work[low:, :]) - update[low:, :]


def factor_kernel(sub, a_ref, out_ref, work, left, right):
    size = a_ref.shape[0]
    count = size // BLOCK
    out_ref[...] = a_ref[...]

    def step(k, carry):
        here = pl.ds(pl.multiple_of(k * BLOCK, BLOCK), BLOCK)
        work[...] = out_ref[here, here]
        eliminate(work, sub)
        r = lax.broadcasted_iota(jnp.int32, (BLOCK, BLOCK), 0)
        c = lax.broadcasted_iota(jnp.int32, (BLOCK, BLOCK), 1)
        inverse = jnp.where(c <= r, work[...], 0.0)
        row = jnp.dot(left6(inverse, 1), right6(out_ref[here, :]), preferred_element_type=jnp.float32)
        out_ref[here, :] = row
        out_ref[here, here] = inverse
        row = out_ref[here, :]
        left[...] = left6(row, 0)
        right[...] = right6(row)

        def trail(i, carry):
            there = pl.ds(pl.multiple_of(i * BLOCK, BLOCK), BLOCK)
            out_ref[there, here] = jnp.zeros((BLOCK, BLOCK), jnp.float32)
            out_ref[there, :] = out_ref[there, :] - dot_t(left[:, there], right[...])
            out_ref[here, there] = jnp.zeros((BLOCK, BLOCK), jnp.float32)
            return carry

        lax.fori_loop(k + 1, count, trail, 0)
        return carry

    lax.fori_loop(0, count, step, 0)


def inverse_factor(diagonal, sub=16):
    size = diagonal.shape[0]
    return pl.pallas_call(
        functools.partial(factor_kernel, sub),
        out_shape=jax.ShapeDtypeStruct((size, size), jnp.float32),
        in_specs=[pl.BlockSpec(memory_space=pltpu.VMEM)],
        out_specs=pl.BlockSpec(memory_space=pltpu.VMEM),
        scratch_shapes=[
            pltpu.VMEM((BLOCK, BLOCK), jnp.float32),
            pltpu.VMEM((6 * BLOCK, size), jnp.bfloat16),
            pltpu.VMEM((6 * BLOCK, size), jnp.bfloat16),
        ],
        compiler_params=pltpu.CompilerParams(vmem_limit_bytes=40 * 1024 * 1024),
        cost_estimate=pl.CostEstimate(flops=2 * 10**9, bytes_accessed=2 * 4 * size * size, transcendentals=0),
    )(diagonal)


def broadcast(value, axis, source):
    kept = jnp.where(lax.axis_index(axis) == source, value, 0).astype(value.dtype)
    return lax.psum(kept, axis)


def body(jacobian, gram_old):
    slab_rows = lax.all_gather(jacobian, "col", axis=1, tiled=True)
    tile_rows = gram_old.shape[0]
    tile_cols = gram_old.shape[1]
    row_index = lax.axis_index("row")
    col_index = lax.axis_index("col")
    col_start = col_index * tile_cols
    owner_row = col_start // tile_rows
    offset = col_start % tile_rows
    own_piece = lax.dynamic_slice_in_dim(slab_rows, offset, tile_cols, 0)
    partner = broadcast(own_piece, "row", owner_row)
    row_ids = row_index * tile_rows + jnp.arange(tile_rows, dtype=jnp.int32)
    col_ids = col_start + jnp.arange(tile_cols, dtype=jnp.int32)
    keep_mask = col_ids[None, :] // PANEL <= row_ids[:, None] // PANEL
    active = col_start // PANEL <= ((row_index + 1) * tile_rows - 1) // PANEL

    def tile_product():
        return lax.dot_general(
            slab_rows, partner, (((1,), (1,)), ((), ())), preferred_element_type=jnp.float32
        )

    def tile_zeros():
        return jnp.zeros((tile_rows, tile_cols), jnp.float32)

    product = lax.cond(active, tile_product, tile_zeros)
    gram_new = jnp.where(keep_mask, gram_old + product / PARAMS, gram_old)
    panel_tiles_count = PANEL // tile_cols
    blocks = []
    for tile_number in range(panel_tiles_count):
        received = broadcast(gram_new, ("row", "col"), tile_number)
        blocks.append(received)
    diagonal = jnp.concatenate(blocks, axis=1)
    diagonal, later = lax.optimization_barrier((diagonal, gram_new))
    inverse = inverse_factor(diagonal)
    own_count = PANEL // lax.axis_size("col")
    pieces = []
    for tile_number in range(panel_tiles_count):
        pieces.append(broadcast(later, "col", tile_number))
    panel_rows = jnp.concatenate(pieces, axis=1)
    own_inverse = lax.dynamic_slice_in_dim(inverse, col_index * own_count, own_count, 0)
    panel_t = lax.dot_general(
        own_inverse,
        panel_rows,
        (((1,), (1,)), ((), ())),
        precision=lax.Precision.HIGHEST,
        preferred_element_type=jnp.float32,
    )
    return (gram_new, panel_t)


def solution(mesh):
    return jax.shard_map(
        body,
        mesh=mesh,
        in_specs=(P("row", "col"), P("row", "col")),
        out_specs=(P("row", "col"), P("col", "row")),
        check_vma=False,
    )
```

```python
import functools
import jax
import jax.numpy as jnp
from jax import lax
from jax.experimental import pallas as pl
from jax.experimental.pallas import tpu as pltpu
from jax.sharding import PartitionSpec as P

PARAMS = 512
PANEL = 1024
BLOCK = 128


def split3(x):
    high = x.astype(jnp.bfloat16).astype(jnp.float32)
    rest = x - high
    mid = rest.astype(jnp.bfloat16).astype(jnp.float32)
    return high, mid, rest - mid


def left6(x, axis):
    h, m, l = split3(x)
    return jnp.concatenate([h, h, m, h, l, m], axis=axis).astype(jnp.bfloat16)


def right6(x):
    h, m, l = split3(x)
    return jnp.concatenate([h, m, h, l, h, m], axis=0).astype(jnp.bfloat16)


def dot_t(a, b):
    return lax.dot_general(a, b, (((0,), (0,)), ((), ())), preferred_element_type=jnp.float32)


def eliminate(work, sub):
    size = work.shape[0]
    lanes = lax.broadcasted_iota(jnp.int32, (sub, size), 1)
    subs = lax.broadcasted_iota(jnp.int32, (sub, size), 0)
    for start in range(0, size, sub):
        rows = work[start:start + sub, :]
        scale = jnp.ones((sub, size), jnp.float32)
        for i in range(sub):
            at = start + i
            column = jnp.broadcast_to(rows[:, at:at + 1], (sub, size))
            pivot = jnp.broadcast_to(column[i:i + 1, :], (sub, size))
            pivot_row = jnp.where(lanes == at, 1.0, jnp.broadcast_to(rows[i:i + 1, :], (sub, size)))
            factor = jnp.where(subs > i, column * (1.0 / pivot), 0.0)
            kept = jnp.where((lanes == at) & (subs >= i), jnp.where(subs == i, 1.0, 0.0), rows)
            rows = kept - factor * pivot_row
            root = lax.rsqrt(pivot)
            root = root * (1.5 - 0.5 * pivot * root * root)
            scale = jnp.where(subs == i, root, scale)
        rows = rows * scale
        work[start:start + sub, :] = rows
        low = start + sub
        if low < size:
            above = (lanes > subs + start) & (lanes < low)
            update = dot_t(left6(rows, 0), right6(jnp.where(above, 0.0, rows)))
            wide = lax.broadcasted_iota(jnp.int32, (size - low, size), 1)
            inside = (wide >= start) & (wide < low)
            work[low:, :] = jnp.where(inside, 0.0, work[low:, :]) - update[low:, :]


def factor_kernel(sub, packed_ref, slab_ref, out_ref, work, left, right):
    size = out_ref.shape[0]
    count = size // BLOCK
    begin = 0
    for j in range(count):
        high = (j + 1) * BLOCK
        part = slice(j * BLOCK, high)
        product = dot_t(slab_ref[:, :high], slab_ref[:, part])
        out_ref[:high, part] = packed_ref[begin:begin + high, :] + product / PARAMS
        if high < size:
            out_ref[high:, part] = jnp.zeros((size - high, BLOCK), jnp.float32)
        begin += high

    def step(k, carry):
        here = pl.ds(pl.multiple_of(k * BLOCK, BLOCK), BLOCK)
        work[...] = out_ref[here, here]
        eliminate(work, sub)
        r = lax.broadcasted_iota(jnp.int32, (BLOCK, BLOCK), 0)
        c = lax.broadcasted_iota(jnp.int32, (BLOCK, BLOCK), 1)
        inverse = jnp.where(c <= r, work[...], 0.0)
        row = jnp.dot(left6(inverse, 1), right6(out_ref[here, :]), preferred_element_type=jnp.float32)
        out_ref[here, :] = row
        out_ref[here, here] = inverse
        row = out_ref[here, :]
        left[...] = left6(row, 0)
        right[...] = right6(row)

        def trail(i, carry):
            there = pl.ds(pl.multiple_of(i * BLOCK, BLOCK), BLOCK)
            out_ref[there, here] = jnp.zeros((BLOCK, BLOCK), jnp.float32)
            out_ref[there, :] = out_ref[there, :] - dot_t(left[:, there], right[...])
            out_ref[here, there] = jnp.zeros((BLOCK, BLOCK), jnp.float32)
            return carry

        lax.fori_loop(k + 1, count, trail, 0)
        return carry

    lax.fori_loop(0, count, step, 0)


def inverse_factor(packed, slab, size, sub=16):
    return pl.pallas_call(
        functools.partial(factor_kernel, sub),
        out_shape=jax.ShapeDtypeStruct((size, size), jnp.float32),
        in_specs=[pl.BlockSpec(memory_space=pltpu.VMEM)] * 2,
        out_specs=pl.BlockSpec(memory_space=pltpu.VMEM),
        scratch_shapes=[
            pltpu.VMEM((BLOCK, BLOCK), jnp.float32),
            pltpu.VMEM((6 * BLOCK, size), jnp.bfloat16),
            pltpu.VMEM((6 * BLOCK, size), jnp.bfloat16),
        ],
        compiler_params=pltpu.CompilerParams(vmem_limit_bytes=40 * 1024 * 1024),
        cost_estimate=pl.CostEstimate(
            flops=100 * 10**9, bytes_accessed=8 * size * size, transcendentals=0
        ),
    )(packed, slab)


def broadcast(value, axis, source):
    kept = jnp.where(lax.axis_index(axis) == source, value, 0).astype(value.dtype)
    return lax.psum(kept, axis)


def pack_upper(tile, tile_number):
    tile_cols = tile.shape[1]
    parts = []
    for begin in range(0, tile_cols, BLOCK):
        high = tile_number * tile_cols + begin + BLOCK
        parts.append(tile[:high, begin:begin + BLOCK])
    return jnp.concatenate(parts, axis=0)


def body(jacobian, gram_old):
    tile_rows, tile_cols = gram_old.shape
    row_index = lax.axis_index("row")
    col_index = lax.axis_index("col")
    panel_tiles_count = PANEL // tile_cols
    place = row_index * lax.axis_size("col") + col_index

    packed = []
    for tile_number in range(panel_tiles_count):
        part = pack_upper(gram_old, tile_number)
        packed.append(jnp.where(place == tile_number, part, 0))
    packed = lax.psum(jnp.concatenate(packed, axis=0), ("row", "col"))

    slabs = lax.all_gather(jacobian.T, ("row", "col"))
    slabs = slabs.reshape(lax.axis_size("row"), PARAMS, tile_rows)
    first = slabs[0][:, :PANEL]
    own = lax.dynamic_index_in_dim(slabs, row_index, 0, keepdims=False)
    col_start = col_index * tile_cols
    partner = lax.dynamic_slice(
        slabs, (col_start // tile_rows, 0, col_start % tile_rows), (1, PARAMS, tile_cols)
    )[0]

    row_ids = row_index * tile_rows + jnp.arange(tile_rows, dtype=jnp.int32)
    col_ids = col_start + jnp.arange(tile_cols, dtype=jnp.int32)
    keep_mask = col_ids[None, :] // PANEL <= row_ids[:, None] // PANEL
    gram_new = jnp.where(keep_mask, gram_old + dot_t(own, partner) / PARAMS, gram_old)

    inverse = inverse_factor(packed, first, PANEL)

    late, own = lax.optimization_barrier((gram_old, own))
    pieces = []
    for tile_number in range(panel_tiles_count):
        pieces.append(broadcast(late, "col", tile_number))
    panel_rows = jnp.concatenate(pieces, axis=1) + dot_t(own, first) / PARAMS
    own_count = PANEL // lax.axis_size("col")
    own_inverse = lax.dynamic_slice_in_dim(inverse, col_index * own_count, own_count, 0)
    panel_t = lax.dot_general(
        own_inverse,
        panel_rows,
        (((1,), (1,)), ((), ())),
        precision=lax.Precision.HIGHEST,
        preferred_element_type=jnp.float32,
    )
    return (gram_new, panel_t)


def solution(mesh):
    return jax.shard_map(
        body,
        mesh=mesh,
        in_specs=(P("row", "col"), P("row", "col")),
        out_specs=(P("row", "col"), P("col", "row")),
        check_vma=False,
    )
```

```python
import functools
import jax
import jax.numpy as jnp
from jax import lax
from jax.experimental import pallas as pl
from jax.experimental.pallas import tpu as pltpu
from jax.sharding import PartitionSpec as P

PARAMS = 512
PANEL = 1024
BLOCK = 128


def split3(x):
    high = x.astype(jnp.bfloat16).astype(jnp.float32)
    rest = x - high
    mid = rest.astype(jnp.bfloat16).astype(jnp.float32)
    return high, mid, rest - mid


def left6(x, axis):
    h, m, l = split3(x)
    return jnp.concatenate([h, h, m, h, l, m], axis=axis).astype(jnp.bfloat16)


def right6(x):
    h, m, l = split3(x)
    return jnp.concatenate([h, m, h, l, h, m], axis=0).astype(jnp.bfloat16)


def dot_t(a, b):
    return lax.dot_general(a, b, (((0,), (0,)), ((), ())), preferred_element_type=jnp.float32)


def eliminate(work, sub):
    size = work.shape[0]
    lanes = lax.broadcasted_iota(jnp.int32, (sub, size), 1)
    subs = lax.broadcasted_iota(jnp.int32, (sub, size), 0)
    for start in range(0, size, sub):
        rows = work[start:start + sub, :]
        scale = jnp.ones((sub, size), jnp.float32)
        for i in range(sub):
            at = start + i
            column = jnp.broadcast_to(rows[:, at:at + 1], (sub, size))
            pivot = jnp.broadcast_to(column[i:i + 1, :], (sub, size))
            pivot_row = jnp.where(lanes == at, 1.0, jnp.broadcast_to(rows[i:i + 1, :], (sub, size)))
            factor = jnp.where(subs > i, column * (1.0 / pivot), 0.0)
            kept = jnp.where((lanes == at) & (subs >= i), jnp.where(subs == i, 1.0, 0.0), rows)
            rows = kept - factor * pivot_row
            root = lax.rsqrt(pivot)
            root = root * (1.5 - 0.5 * pivot * root * root)
            scale = jnp.where(subs == i, root, scale)
        rows = rows * scale
        work[start:start + sub, :] = rows
        low = start + sub
        if low < size:
            above = (lanes > subs + start) & (lanes < low)
            update = dot_t(left6(rows, 0), right6(jnp.where(above, 0.0, rows)))
            wide = lax.broadcasted_iota(jnp.int32, (size - low, size), 1)
            inside = (wide >= start) & (wide < low)
            work[low:, :] = jnp.where(inside, 0.0, work[low:, :]) - update[low:, :]


def factor_kernel(sub, packed_ref, slab_ref, out_ref, work, left, right):
    size = out_ref.shape[0]
    count = size // BLOCK
    begin = 0
    for j in range(count):
        high = (j + 1) * BLOCK
        part = slice(j * BLOCK, high)
        product = dot_t(slab_ref[:, :high], slab_ref[:, part])
        out_ref[:high, part] = packed_ref[begin:begin + high, :] + product / PARAMS
        if high < size:
            out_ref[high:, part] = jnp.zeros((size - high, BLOCK), jnp.float32)
        begin += high

    def step(k, carry):
        here = pl.ds(pl.multiple_of(k * BLOCK, BLOCK), BLOCK)
        work[...] = out_ref[here, here]
        eliminate(work, sub)
        r = lax.broadcasted_iota(jnp.int32, (BLOCK, BLOCK), 0)
        c = lax.broadcasted_iota(jnp.int32, (BLOCK, BLOCK), 1)
        inverse = jnp.where(c <= r, work[...], 0.0)
        row = jnp.dot(left6(inverse, 1), right6(out_ref[here, :]), preferred_element_type=jnp.float32)
        out_ref[here, :] = row
        out_ref[here, here] = inverse
        row = out_ref[here, :]
        left[...] = left6(row, 0)
        right[...] = right6(row)

        def trail(i, carry):
            there = pl.ds(pl.multiple_of(i * BLOCK, BLOCK), BLOCK)
            out_ref[there, here] = jnp.zeros((BLOCK, BLOCK), jnp.float32)
            out_ref[there, :] = out_ref[there, :] - dot_t(left[:, there], right[...])
            out_ref[here, there] = jnp.zeros((BLOCK, BLOCK), jnp.float32)
            return carry

        lax.fori_loop(k + 1, count, trail, 0)
        return carry

    lax.fori_loop(0, count, step, 0)


def inverse_factor(packed, slab, size, sub=16):
    return pl.pallas_call(
        functools.partial(factor_kernel, sub),
        out_shape=jax.ShapeDtypeStruct((size, size), jnp.float32),
        in_specs=[pl.BlockSpec(memory_space=pltpu.VMEM)] * 2,
        out_specs=pl.BlockSpec(memory_space=pltpu.VMEM),
        scratch_shapes=[
            pltpu.VMEM((BLOCK, BLOCK), jnp.float32),
            pltpu.VMEM((6 * BLOCK, size), jnp.bfloat16),
            pltpu.VMEM((6 * BLOCK, size), jnp.bfloat16),
        ],
        compiler_params=pltpu.CompilerParams(vmem_limit_bytes=40 * 1024 * 1024),
        cost_estimate=pl.CostEstimate(
            flops=100 * 10**9, bytes_accessed=8 * size * size, transcendentals=0
        ),
    )(packed, slab)


def broadcast(value, axis, source):
    kept = jnp.where(lax.axis_index(axis) == source, value, 0).astype(value.dtype)
    return lax.psum(kept, axis)


def pack_upper(tile, tile_number):
    tile_cols = tile.shape[1]
    parts = []
    for begin in range(0, tile_cols, BLOCK):
        high = tile_number * tile_cols + begin + BLOCK
        parts.append(tile[:high, begin:begin + BLOCK])
    return jnp.concatenate(parts, axis=0)


def body(jacobian, gram_old):
    tile_rows, tile_cols = gram_old.shape
    row_index = lax.axis_index("row")
    col_index = lax.axis_index("col")
    panel_tiles_count = PANEL // tile_cols

    packed = []
    for tile_number in range(panel_tiles_count):
        part = pack_upper(gram_old, tile_number)
        packed.append(jnp.where(col_index == tile_number, part, 0))
    packed = jnp.concatenate(packed, axis=0)
    packed = packed.reshape(lax.axis_size("col"), -1, BLOCK)
    share = lax.all_to_all(packed, "col", 0, 0)
    share = jnp.sum(share[:panel_tiles_count], axis=0)
    share = broadcast(share, "row", 0)
    packed = lax.all_gather(share, "col", axis=0, tiled=True)

    slabs = lax.all_gather(jacobian.T, ("row", "col"))
    slabs = slabs.reshape(lax.axis_size("row"), PARAMS, tile_rows)
    first = slabs[0][:, :PANEL]
    own = lax.dynamic_index_in_dim(slabs, row_index, 0, keepdims=False)
    col_start = col_index * tile_cols
    partner = lax.dynamic_slice(
        slabs, (col_start // tile_rows, 0, col_start % tile_rows), (1, PARAMS, tile_cols)
    )[0]

    row_ids = row_index * tile_rows + jnp.arange(tile_rows, dtype=jnp.int32)
    col_ids = col_start + jnp.arange(tile_cols, dtype=jnp.int32)
    keep_mask = col_ids[None, :] // PANEL <= row_ids[:, None] // PANEL
    gram_new = jnp.where(keep_mask, gram_old + dot_t(own, partner) / PARAMS, gram_old)

    inverse = inverse_factor(packed, first, PANEL)

    late, own = lax.optimization_barrier((gram_old, own))
    pieces = []
    for tile_number in range(panel_tiles_count):
        pieces.append(broadcast(late, "col", tile_number))
    panel_rows = jnp.concatenate(pieces, axis=1) + dot_t(own, first) / PARAMS
    own_count = PANEL // lax.axis_size("col")
    own_inverse = lax.dynamic_slice_in_dim(inverse, col_index * own_count, own_count, 0)
    panel_t = lax.dot_general(
        own_inverse,
        panel_rows,
        (((1,), (1,)), ((), ())),
        precision=lax.Precision.HIGHEST,
        preferred_element_type=jnp.float32,
    )
    return (gram_new, panel_t)


def solution(mesh):
    return jax.shard_map(
        body,
        mesh=mesh,
        in_specs=(P("row", "col"), P("row", "col")),
        out_specs=(P("row", "col"), P("col", "row")),
        check_vma=False,
    )
```
